256 devices in a mesh: occ: 4 (over y), vir: 32 (over z, x), pair: 2 (over core).
Axes of the slice: x: 4, y: 4, z: 8, core: 2. Of those that a mesh axis runs over, the one named last changes fastest.
Arguments:
- amplitudes: bfloat16 [2, 4096, 8192], P('pair', 'occ', 'vir'), may hold values from -6 to 6
- hh_integrals: bfloat16 [2, 4096, 4096], P('pair', 'occ'), may hold values from -0.09375 to 0.09375
- ladder_blocks: bfloat16 [32, 64, 128, 128], P('vir'), may hold values from -0.09375 to 0.09375
- block_target: int32 [32, 64], P('vir'), may hold values from 0 to 63, each once within a row
- block_live: int32 [32, 64], P('vir'), may hold values from 0 to 1
Outputs:
- residual: bfloat16 [2, 4096, 8192], P('pair', 'occ', 'vir')
The draws below stay inside these ranges and needn't reach their ends.
Inputs may be any that keep to these rules, and one draw needn't show every extreme that they name: `block_target`: each row is a permutation: the 64 blocks of one index of vir reach every tile exactly once.
All inputs are finite; a program needn't handle non-finite values.
Results may differ from the reference program's by a relative error of at most 0.0037.
Values may be sent and summed in bfloat16 or wider, within the bound.
A program may use at most 128 MiB of HBM per device.

```python
import jax
import jax.numpy as jnp
from jax import lax

TILE = 128
TL_DEV = 2
NOP = 4096
NT = 64
N_VIR = 32


def draw_block_live(key, part):
    key = jax.random.fold_in(key, 7)
    level_key, roll_key = jax.random.split(key)
    levels = jax.random.randint(level_key, (N_VIR, 1), 1, 5)
    rolled = jax.random.randint(roll_key, (N_VIR, NT), 0, 4)
    return (rolled < levels).astype(jnp.int32)


def steps_of(stream_key, shape, cuts, least, largest):
    def one(dim, parts):
        draws = jax.random.uniform(jax.random.fold_in(jax.random.fold_in(stream_key, 6), dim), (parts,), jnp.float32, least / len(cuts), largest / len(cuts))
        return jnp.repeat(jnp.exp(draws), shape[dim] // parts).reshape((-1,) + (1,) * (len(shape) - dim - 1))

    factor_of = one(*cuts[0])
    for cut in cuts[1:]:
        factor_of = factor_of * one(*cut)
    return factor_of


def bell_draw(key, dims, deviation, limit, cuts=(), kind=jnp.bfloat16):
    array = jax.random.normal(key, dims, jnp.float32) * deviation
    if len(cuts) > 0:
        array = steps_of(key, dims, cuts, -0.22, 0.18) * array
    return jnp.clip(array, min=-limit, max=limit).astype(kind)


def setup_inputs(seed: int = 0) -> dict:
    keys = jax.random.split(jax.random.key(seed), 6)
    return {
        "amplitudes": bell_draw(keys[0], (2, NOP, NT * TILE), 1.0, 6.0, ((0, 2), (1, 4), (2, 32))),
        "hh_integrals": bell_draw(keys[1], (2, NOP, NOP), NOP ** -0.5, 0.09375, ((0, 2), (1, 4))),
        "ladder_blocks": bell_draw(keys[2], (N_VIR, NT, TILE, TILE), (TILE * N_VIR) ** -0.5, 0.09375, ((0, 32),)),
        "block_target": jax.vmap(lambda own: jax.random.permutation(own, NT))(jax.random.split(keys[3], N_VIR)).reshape((N_VIR, NT)).astype(jnp.int32),
        "block_live": draw_block_live(jax.random.fold_in(keys[5], 71), 0),
    }


def reference(amplitudes, hh_integrals, ladder_blocks, block_target, block_live):
    col_span = TL_DEV * TILE

    def source_step(running, source):
        grouped = ladder_blocks[source].reshape(TL_DEV, N_VIR, TILE, TILE).astype(jnp.float32)
        live_mask = block_live[source].reshape(TL_DEV, N_VIR).astype(jnp.bfloat16)
        for half in range(2):
            tile_view = lax.dynamic_slice_in_dim(amplitudes[half], (source * col_span).astype(jnp.int32), col_span, 1)
            tile_view = tile_view.reshape(NOP, TL_DEV, TILE)
            partials = jnp.einsum("pyc,ykcd->ykpd", tile_view.astype(jnp.float32), grouped).astype(jnp.bfloat16)
            partials = partials * live_mask[:, :, None, None]
            partials = partials.reshape(NT, NOP, TILE)
            running = running.at[block_target[source]].add(partials.astype(jnp.float32))
        return running, None

    start_sum = jnp.zeros((NT, NOP, TILE), jnp.float32)
    total, unused = lax.scan(source_step, start_sum, jnp.arange(N_VIR, dtype=jnp.int32))
    ladder = total.transpose(1, 0, 2).reshape(NOP, NT * TILE)
    hole_term = jnp.einsum("mpq,mqc->mpc", hh_integrals.astype(jnp.float32), amplitudes.astype(jnp.float32))
    symmetric = (ladder + hole_term[0] + hole_term[1]).astype(jnp.bfloat16)
    return jnp.stack([symmetric, symmetric])
```

```python
import jax
import jax.numpy as jnp
from jax import lax
from jax.experimental import pallas as pl
from jax.experimental.pallas import tpu as pltpu
from jax.sharding import PartitionSpec as P

MESH = pl.DeviceIdType.MESH
TILE = 128
NX = 4
NY = 4
NZ = 8
NT = 64
ROWS = 1024
HALF = 512
COLS = 256
CH = 128
NC = HALF // CH
F32 = jnp.float32
BF16 = jnp.bfloat16


def kernel(inv, live, amp, hh, blocks, out,
           amp_v, aoth, s_all, a_all, h_v, l_raw, l_own, l_in, meta_own, meta_in,
           l_dense, zs, zr, acc, hx, fin, ofin,
           sem_lraw, sem_amp, sem_h, pa_s, pa_r, ya_s, ya_r, xs_s, xs_r, xl_s, xl_r,
           xm_s, xm_r, pl_s, pl_r, z_s, z_r, ph_s, ph_r, po_s, po_r, lo_s):
    y = lax.axis_index("occ")
    v = lax.axis_index("vir")
    p = lax.axis_index("pair")
    z = v // NX
    x = v % NX

    def at_x(dx):
        return {"occ": y, "vir": z * NX + (x + dx) % NX, "pair": p}

    def at_y(dy):
        return {"occ": (y + dy) % NY, "vir": v, "pair": p}

    def at_z(dz):
        return {"occ": y, "vir": ((z + dz) % NZ) * NX + x, "pair": p}

    mate = {"occ": y, "vir": v, "pair": 1 - p}

    def remote(src, dst, ss, rs, dev):
        return pltpu.make_async_remote_copy(
            src_ref=src, dst_ref=dst, send_sem=ss, recv_sem=rs,
            device_id=dev, device_id_type=MESH)

    def crow(c):
        return pl.ds(pl.multiple_of(c * CH, CH), CH)

    get_lraw = pltpu.make_async_copy(blocks.at[0], l_raw, sem_lraw)
    get_amp = pltpu.make_async_copy(amp.at[0], amp_v, sem_amp)
    get_h = [
        pltpu.make_async_copy(
            hh.at[0, :, pl.ds(pl.multiple_of(((y + k) % NY) * ROWS, ROWS), ROWS)],
            h_v.at[k], sem_h.at[k])
        for k in range(NY)
    ]
    get_lraw.start()
    get_amp.start()
    for g in get_h:
        g.start()

    barrier = pltpu.get_barrier_semaphore()
    peers = [at_x(1), at_x(2), at_x(3), at_y(1), at_y(2), at_y(3), at_z(1), at_z(NZ - 1), mate]
    for dev in peers:
        pl.semaphore_signal(barrier, inc=1, device_id=dev, device_id_type=MESH)

    get_lraw.wait()

    def sort_block(i, carry):
        d = i // 8
        t = (i // 4) % 2
        dx = i % 4
        tile = 2 * (((z + d) % NZ) * NX + (x + dx) % NX) + t
        r = inv[tile]
        l_own[d, t, dx] = l_raw[r]
        alive = live[r].astype(F32)
        upper = jnp.where(r < NT // 2, alive, 0.0)
        row = d * 4 + t * 2
        meta_own[dx, pl.ds(row, 1), :] = jnp.full((1, TILE), upper, F32)
        meta_own[dx, pl.ds(row + 1, 1), :] = jnp.full((1, TILE), alive - upper, F32)
        return carry

    lax.fori_loop(0, NT, sort_block, 0)
    pl.semaphore_wait(barrier, len(peers))

    def pair_amp(c):
        return remote(
            amp.at[0, pl.ds(pl.multiple_of((1 - p) * HALF + c * CH, CH), CH)],
            aoth.at[crow(c)], pa_s.at[c], pa_r.at[c], mate)

    def y_amp(dy):
        return remote(amp.at[0], a_all.at[NY - dy - 1], ya_s.at[dy - 1], ya_r.at[NY - dy - 1], at_y(dy))

    def x_meta(dx):
        return remote(meta_own.at[dx], meta_in.at[NX - dx - 1], xm_s.at[dx - 1], xm_r.at[NX - dx - 1], at_x(dx))

    def x_block(d, dx):
        return remote(l_own.at[d, p, dx], l_in.at[d, p, NX - dx - 1],
                      xl_s.at[d, dx - 1], xl_r.at[d, NX - dx - 1], at_x(dx))

    def x_sum(c, dx):
        return remote(s_all.at[0, crow(c)], s_all.at[NX - dx, crow(c)],
                      xs_s.at[c, dx - 1], xs_r.at[c, NX - dx - 1], at_x(dx))

    def pair_block(d):
        return remote(l_in.at[d, p], l_in.at[d, p], pl_s.at[d], pl_r.at[d], mate)

    ORDER = (1, 3, 2)
    for c in range(NC):
        pair_amp(c).start()
    for dx in ORDER:
        x_meta(dx).start()
        x_block(4, dx).start()
    for dy in ORDER:
        y_amp(dy).start()
    get_amp.wait()

    def send_sum(c):
        pair_amp(c).wait_recv()
        mine = amp_v[pl.ds(pl.multiple_of(p * HALF + c * CH, CH), CH), :]
        s_all[0, crow(c), :] = (mine.astype(F32) + aoth[crow(c), :].astype(F32)).astype(BF16)
        for dx in ORDER:
            x_sum(c, dx).start()

    def send_blocks(*ds):
        for d in ds:
            for dx in ORDER:
                x_block(d, dx).start()

    send_sum(0)
    send_sum(1)
    send_blocks(3, 5)
    send_sum(2)
    send_sum(3)
    send_blocks(2, 6, 1, 7, 0)

    def hole(k, a_ref, first):
        def step(i, carry):
            rows = pl.ds(pl.multiple_of(i * 256, 256), 256)
            term = jnp.dot(h_v[k, rows, :], a_ref[...], preferred_element_type=F32)
            if first:
                acc[rows, :] = term
            else:
                acc[rows, :] += term
            return carry
        lax.fori_loop(0, ROWS // 256, step, 0)

    def gather_blocks(*ds):
        for d in ds:
            for dx in ORDER:
                x_block(d, dx).wait_recv()
            pair_block(d).start()
        for d in ds:
            pltpu.make_async_remote_copy(
                src_ref=l_in.at[d, 1 - p], dst_ref=l_in.at[d, 1 - p], send_sem=pl_s.at[d],
                recv_sem=pl_r.at[d], device_id=mate, device_id_type=MESH).wait_recv()
            for k in range(NX):
                for t in range(2):
                    row = d * 4 + t * 2
                    if k == 0:
                        block = l_own[d, t, 0]
                        m0 = meta_own[0, row:row + 1, :]
                        m1 = meta_own[0, row + 1:row + 2, :]
                    else:
                        block = l_in[d, t, k - 1]
                        m0 = meta_in[k - 1, row:row + 1, :]
                        m1 = meta_in[k - 1, row + 1:row + 2, :]
                    cols = slice(t * TILE, (t + 1) * TILE)
                    l_dense[d, k * 256:k * 256 + 128, cols] = block * m0.astype(BF16)
                    l_dense[d, k * 256 + 128:k * 256 + 256, cols] = block * m1.astype(BF16)

    def product(c, d):
        total = jnp.dot(s_all[0, crow(c), :], l_dense[d, 0:256, :], preferred_element_type=F32)
        for k in range(1, NX):
            total += jnp.dot(s_all[k, crow(c), :], l_dense[d, k * 256:(k + 1) * 256, :],
                             preferred_element_type=F32)
        return total

    def z_rows(h, c):
        size = CH // 2 if h == 0 else CH
        return pl.ds(pl.multiple_of(c * size, size), size)

    def z_copy(way, h, c):
        rows = z_rows(h, c)
        return remote(zs.at[way, h, rows], zr.at[way, h, rows], z_s.at[way, h, c], z_r.at[way, h, c],
                      at_z(1 if way == 0 else NZ - 1))

    def z_step(h, c):
        if h == 0:
            for dx in ORDER:
                x_sum(c, dx).wait_recv()
            total = product(c, 4)
            for way in range(2):
                zs[way, 0, z_rows(0, c), :] = total[way * 64:(way + 1) * 64].astype(BF16)
                z_copy(way, 0, c).start()
            return
        for way in range(2):
            total = product(c, 4 - h if way == 0 else 4 + h)
            z_copy(way, h - 1, c).wait_recv()
            got = zr[way, h - 1, z_rows(h - 1, c), :].astype(F32)
            if h == 1:
                lo = pl.ds(pl.multiple_of(c * CH, CH), 64)
                hi = pl.ds(pl.multiple_of(c * CH + 64, 64), 64)
                if way == 0:
                    zs[way, h, lo, :] = (total[:64] + got).astype(BF16)
                    zs[way, h, hi, :] = total[64:].astype(BF16)
                else:
                    zs[way, h, lo, :] = total[:64].astype(BF16)
                    zs[way, h, hi, :] = (total[64:] + got).astype(BF16)
            else:
                zs[way, h, crow(c), :] = (total + got).astype(BF16)
            z_copy(way, h, c).start()

    def z_steps(lo, hi, *hs):
        def step(c, carry):
            for h in hs:
                z_step(h, c)
            return carry
        lax.fori_loop(lo, hi, step, 0)

    get_h[0].wait()
    hole(0, amp_v, True)
    for dx in ORDER:
        x_meta(dx).wait_recv()
    gather_blocks(4)
    z_steps(0, 2, 0)
    gather_blocks(3, 5)
    z_steps(0, 2, 1)
    z_steps(2, 4, 0, 1)
    for k in (1, 3):
        get_h[k].wait()
        y_amp(NY - k).wait_recv()
        hole(k, a_all.at[k - 1], False)
    gather_blocks(2, 6)
    z_steps(0, 4, 2)
    gather_blocks(1, 7)
    z_steps(0, 4, 3)
    get_h[2].wait()
    y_amp(2).wait_recv()
    hole(2, a_all.at[1], False)
    pair_hole = remote(
        acc.at[pl.ds(pl.multiple_of((1 - p) * HALF, HALF), HALF)], hx, ph_s, ph_r, mate)
    pair_hole.start()
    gather_blocks(0)

    def own_product(c, carry):
        fin[crow(c), :] = product(c, 0)
        return carry

    lax.fori_loop(0, NC, own_product, 0)
    pair_hole.wait_recv()

    def out_copies(c):
        rows = pl.ds(pl.multiple_of(p * HALF + c * CH, CH), CH)
        return (
            pltpu.make_async_copy(ofin.at[crow(c)], out.at[0, rows], lo_s.at[c]),
            remote(ofin.at[crow(c)], out.at[0, rows], po_s.at[c], po_r.at[c], mate),
        )

    def finish(c, carry):
        z_copy(0, 3, c).wait_recv()
        z_copy(1, 3, c).wait_recv()
        rows = pl.ds(pl.multiple_of(p * HALF + c * CH, CH), CH)
        total = fin[crow(c), :] + acc[rows, :] + hx[crow(c), :]
        total += zr[0, 3, crow(c), :].astype(F32) + zr[1, 3, crow(c), :].astype(F32)
        ofin[crow(c), :] = total.astype(BF16)
        for copy in out_copies(c):
            copy.start()
        return carry

    lax.fori_loop(0, NC, finish, 0)

    pair_hole.wait_send()
    for dx in ORDER:
        x_meta(dx).wait_send()
        y_amp(dx).wait_send()

    def drain_d(d, carry):
        for dx in ORDER:
            x_block(d, dx).wait_send()
        pair_block(d).wait_send()
        return carry

    lax.fori_loop(0, NZ, drain_d, 0)

    def drain_c(c, carry):
        pair_amp(c).wait_send()
        for dx in ORDER:
            x_sum(c, dx).wait_send()
        for way in range(2):
            for h in range(4):
                z_copy(way, h, c).wait_send()
        keep, give = out_copies(c)
        keep.wait()
        give.wait()
        return carry

    lax.fori_loop(0, NC, drain_c, 0)


def on_device(amplitudes, hh_integrals, ladder_blocks, block_target, block_live):
    index = jnp.arange(NT, dtype=jnp.int32)
    hit = block_target[0][None, :] == index[:, None]
    inverse = jnp.sum(jnp.where(hit, index[None, :], 0), axis=1)
    dma = pltpu.SemaphoreType.DMA
    any_space = pl.BlockSpec(memory_space=pl.ANY)
    smem = pl.BlockSpec(memory_space=pltpu.SMEM)
    return pl.pallas_call(
        kernel,
        out_shape=jax.ShapeDtypeStruct((1, ROWS, COLS), BF16),
        in_specs=[smem, smem, any_space, any_space, any_space],
        out_specs=any_space,
        scratch_shapes=[
            pltpu.VMEM((ROWS, COLS), BF16),
            pltpu.VMEM((HALF, COLS), BF16),
            pltpu.VMEM((NX, HALF, COLS), BF16),
            pltpu.VMEM((NY - 1, ROWS, COLS), BF16),
            pltpu.VMEM((NY, ROWS, ROWS), BF16),
            pltpu.VMEM((NT, TILE, TILE), BF16),
            pltpu.VMEM((NZ, 2, NX, TILE, TILE), BF16),
            pltpu.VMEM((NZ, 2, NX - 1, TILE, TILE), BF16),
            pltpu.VMEM((NX, 4 * NZ, TILE), F32),
            pltpu.VMEM((NX - 1, 4 * NZ, TILE), F32),
            pltpu.VMEM((NZ, NX * COLS, COLS), BF16),
            pltpu.VMEM((2, 4, HALF, COLS), BF16),
            pltpu.VMEM((2, 4, HALF, COLS), BF16),
            pltpu.VMEM((ROWS, COLS), F32),
            pltpu.VMEM((HALF, COLS), F32),
            pltpu.VMEM((HALF, COLS), F32),
            pltpu.VMEM((HALF, COLS), BF16),
            dma, dma, dma((NY,)),
            dma((NC,)), dma((NC,)),
            dma((NY - 1,)), dma((NY - 1,)),
            dma((NC, NX - 1)), dma((NC, NX - 1)),
            dma((NZ, NX - 1)), dma((NZ, NX - 1)),
            dma((NX - 1,)), dma((NX - 1,)),
            dma((NZ,)), dma((NZ,)),
            dma((2, 4, NC)), dma((2, 4, NC)),
            dma, dma,
            dma((NC,)), dma((NC,)),
            dma((NC,)),
        ],
        compiler_params=pltpu.CompilerParams(
            collective_id=0, has_side_effects=True, vmem_limit_bytes=56 * 2**20),
        cost_estimate=pl.CostEstimate(
            flops=4 * ROWS * 4096 * COLS, bytes_accessed=12 * 2**20, transcendentals=0),
        name="ladder_hole",
    )(inverse, block_live[0], amplitudes, hh_integrals, ladder_blocks)


def solution(mesh):
    return jax.shard_map(
        on_device,
        mesh=mesh,
        in_specs=(
            P("pair", "occ", "vir"),
            P("pair", "occ", None),
            P("vir", None, None, None),
            P("vir", None),
            P("vir", None),
        ),
        out_specs=P("pair", "occ", "vir"),
        check_vma=False,
    )
```

```python
import jax
import jax.numpy as jnp
from jax import lax
from jax.experimental import pallas as pl
from jax.experimental.pallas import tpu as pltpu
from jax.sharding import PartitionSpec as P

MESH = pl.DeviceIdType.MESH
TILE = 128
NX = 4
NY = 4
NZ = 8
NT = 64
ROWS = 1024
HALF = 512
COLS = 256
CH = 128
NC = HALF // CH
NP = 4
PIECE = ROWS // NP
DIRECT = (4,)
SHARED = (3, 5)

PLAN = (
    ("LX", 3), ("LX", 5), ("LS", 4), ("SS", 1), ("LY", 5), ("SS", 3), ("LY", 3), ("SS", 0), ("META",),
    ("LZ", 5), ("LZ", 3), ("LP", 4), ("SH", 1), ("YS", 1), ("SH", 3), ("LS", 6), ("LP", 3), ("SH", 0),
    ("SS", 2), ("LB", 4), ("LS", 2), ("Z", 0, 3), ("LP", 5), ("LS", 0), ("YS", 3), ("LH", 6), ("Z", 0, 0),
    ("Z", 0, 1), ("SH", 2), ("LB", 3), ("LB", 5), ("Z", 1, 3), ("YS", 2), ("LH", 2), ("YS", 0), ("LS", 7),
    ("Z", 1, 0), ("LH", 0), ("LP", 6), ("YP", 1), ("LS", 1), ("Z", 0, 2), ("LP", 2), ("Z", 1, 1), ("LH", 7),
    ("LP", 0), ("LB", 6), ("LB", 2), ("Z", 2, 3), ("LH", 1), ("Z", 1, 2), ("YP", 3), ("Z", 2, 0), ("LP", 7),
    ("HO", 0), ("YP", 0), ("Z", 2, 1), ("LP", 1), ("HO", 2), ("LB", 0), ("OP",), ("YP", 2), ("Z", 2, 2),
    ("LB", 7), ("HO", 1), ("LB", 1), ("Z", 3, 0), ("Z", 3, 3), ("Z", 3, 2), ("HO", 3), ("Z", 3, 1), ("PH",),
    ("FIN", 2), ("FIN", 3), ("FIN", 0), ("FIN", 1),
)
F32 = jnp.float32
BF16 = jnp.bfloat16


def kernel(target, live, amp, hh, blocks, out,
           amp_v, aoth, s_all, a_all, h_v, l_raw, l_own, l_in, l_via, meta_own, meta_in, target_v, live_v, code_v, code,
           l_dense, zs, zr, acc, hx, fin,
           sem_target, sem_live, sem_lraw, sem_amp, sem_code, sem_h, pa_s, pa_r, ya_s, ya_r, xs_s, xs_r, xl_s, xl_r, yl_s, yl_r,
           xm_s, xm_r, pl_s, pl_r, z_s, z_r, ph_s, ph_r, po_s, po_r):
    y = lax.axis_index("occ")
    v = lax.axis_index("vir")
    p = lax.axis_index("pair")
    z = v // NX
    x = v % NX
    far = 1 + 2 * p

    def at_x(dx):
        return {"occ": y, "vir": z * NX + (x + dx) % NX, "pair": p}

    def at_y(dy):
        return {"occ": (y + dy) % NY, "vir": v, "pair": p}

    def at_z(dz):
        return {"occ": y, "vir": ((z + dz) % NZ) * NX + x, "pair": p}

    mate = {"occ": y, "vir": v, "pair": 1 - p}

    def remote(src, dst, ss, rs, dev):
        return pltpu.make_async_remote_copy(
            src_ref=src, dst_ref=dst, send_sem=ss, recv_sem=rs,
            device_id=dev, device_id_type=MESH)

    def crow(c):
        return pl.ds(pl.multiple_of(c * CH, CH), CH)

    barrier = pltpu.get_barrier_semaphore()
    peers = [at_x(1), at_x(2), at_x(3), at_y(1), at_y(3), at_z(1), at_z(NZ - 1), mate]
    for dev in peers:
        pl.semaphore_signal(barrier, inc=1, device_id=dev, device_id_type=MESH)

    get_lraw = pltpu.make_async_copy(blocks.at[0], l_raw, sem_lraw)
    get_amp = pltpu.make_async_copy(amp.at[0], amp_v, sem_amp)
    get_h = [
        pltpu.make_async_copy(
            hh.at[0, :, pl.ds(pl.multiple_of(((y + k) % NY) * ROWS, ROWS), ROWS)],
            h_v.at[k], sem_h.at[k])
        for k in range(NY)
    ]
    get_target = pltpu.make_async_copy(target, target_v, sem_target)
    get_live = pltpu.make_async_copy(live, live_v, sem_live)
    get_target.start()
    get_live.start()
    get_lraw.start()
    get_amp.start()
    get_target.wait()
    get_live.wait()

    entry = lax.broadcasted_iota(jnp.int32, (NT, NT), 1)
    hit = jnp.broadcast_to(target_v[...], (NT, NT)) == lax.broadcasted_iota(jnp.int32, (NT, NT), 0)
    value = 2 * entry + jnp.broadcast_to(live_v[...], (NT, NT))
    found = jnp.max(jnp.where(hit, value, 0), axis=1, keepdims=True)
    code_v[...] = jnp.broadcast_to(found, (NT, TILE))
    get_code = pltpu.make_async_copy(code_v, code, sem_code)
    get_code.start()

    def sort_blocks(*ds):
        for d in ds:
            for t in range(2):
                for dx in range(NX):
                    tile = 2 * (((z + d) % NZ) * NX + (x + dx) % NX) + t
                    l_own[d, t, dx] = l_raw[code[tile, 0] // 2]

    def sort_meta(i, carry):
        d = i // 8
        t = (i // 4) % 2
        dx = i % 4
        tile = 2 * (((z + d) % NZ) * NX + (x + dx) % NX) + t
        both = code[tile, 0]
        alive = (both % 2).astype(F32)
        upper = jnp.where(both < NT, alive, 0.0)
        row = d * 4 + t * 2
        meta_own[dx, pl.ds(row, 1), :] = jnp.full((1, TILE), upper, F32)
        meta_own[dx, pl.ds(row + 1, 1), :] = jnp.full((1, TILE), alive - upper, F32)
        return carry

    pl.semaphore_wait(barrier, len(peers))

    def pair_amp(c):
        return remote(
            amp.at[0, pl.ds(pl.multiple_of((1 - p) * HALF + c * CH, CH), CH)],
            aoth.at[crow(c)], pa_s.at[c], pa_r.at[c], mate)

    def y_amp(j, i):
        rows = pl.ds(j * PIECE, PIECE)
        return remote(amp.at[0, rows], a_all.at[2 - 2 * i, rows], ya_s.at[j, i], ya_r.at[j, i], at_y(1 + 2 * i))

    def y_hop(j):
        rows = pl.ds(j * PIECE, PIECE)
        return remote(a_all.at[2 - 2 * p, rows], a_all.at[1, rows], ya_s.at[j, 2], ya_r.at[j, 2], at_y(far))

    def x_meta(i):
        return remote(meta_own.at[1 + 2 * i], meta_in.at[2 - 2 * i], xm_s.at[i], xm_r.at[i], at_x(1 + 2 * i))

    def x_meta_two():
        return remote(meta_own.at[2], meta_in.at[1], xm_s.at[2], xm_r.at[2], at_x(2))

    def x_block(d, i):
        return remote(l_own.at[d, p, 1 + 2 * i], l_in.at[d, p, 2 - 2 * i],
                      xl_s.at[d, i], xl_r.at[d, i], at_x(1 + 2 * i))

    def x_via(d):
        return remote(l_own.at[d, p, 2], l_via.at[d], xl_s.at[d, 2], xl_r.at[d, 2], at_x(far))

    def x_two(d):
        return remote(l_own.at[d, p, 2], l_in.at[d, p, 1], xl_s.at[d, 3], xl_r.at[d, 3], at_x(2))

    def x_hop(d):
        if d in DIRECT:
            return x_two(d)
        return remote(l_via.at[d], l_in.at[d, p, 1], xl_s.at[d, 3], xl_r.at[d, 3], at_x(far))

    def x_sum(c, i):
        return remote(s_all.at[0, crow(c)], s_all.at[3 - 2 * i, crow(c)],
                      xs_s.at[c, i], xs_r.at[c, i], at_x(1 + 2 * i))

    def x_sum_hop(c):
        return remote(s_all.at[3 - 2 * p, crow(c)], s_all.at[2, crow(c)],
                      xs_s.at[c, 2], xs_r.at[c, 2], at_x(far))

    def pair_block(d):
        return remote(l_in.at[d, p], l_in.at[d, p], pl_s.at[d], pl_r.at[d], mate)

    def send_blocks(*ds):
        for d in ds:
            if d in DIRECT:
                x_two(d).start()
            else:
                x_via(d).start()
            x_block(d, 0).start()
            x_block(d, 1).start()

    def hop_blocks(*ds):
        for d in ds:
            x_via(d).wait_recv()
            x_hop(d).start()

    def send_sum(c):
        pair_amp(c).wait_recv()
        mine = amp_v[pl.ds(pl.multiple_of(p * HALF + c * CH, CH), CH), :]
        s_all[0, crow(c), :] = (mine.astype(F32) + aoth[crow(c), :].astype(F32)).astype(BF16)
        x_sum(c, 0).start()
        x_sum(c, 1).start()

    def hop_sum(c):
        x_sum(c, p).wait_recv()
        x_sum_hop(c).start()

    def hole(k, a_ref, first):
        def step(i, carry):
            rows = pl.ds(pl.multiple_of(i * 256, 256), 256)
            term = jnp.dot(h_v[k, rows, :], a_ref[...], preferred_element_type=F32)
            if first:
                acc[rows, :] = term
            else:
                acc[rows, :] += term
            return carry
        lax.fori_loop(0, ROWS // 256, step, 0)

    def quarter(q):
        return pl.ds(pl.multiple_of((q % NY) * 32, 32), 32)

    def x_share(d, dx):
        return remote(l_own.at[d, p, dx, quarter(y)], l_in.at[d, p, NX - dx - 1, quarter(y)],
                      xl_s.at[d, dx - 1], xl_r.at[d, NX - dx - 1], at_x(dx))

    def y_share(d, i):
        return remote(l_in.at[d, p, :, quarter(y)], l_in.at[d, p, :, quarter(y)],
                      yl_s.at[d, i], yl_r.at[d, i], at_y(1 + 2 * i))

    def y_share_in(d, i):
        part = l_in.at[d, p, :, quarter(y + 3 - 2 * i)]
        return remote(part, part, yl_s.at[d, i], yl_r.at[d, i], at_y(1 + 2 * i))

    def y_share_hop(d):
        part = l_in.at[d, p, :, quarter(y + 3 - 2 * p)]
        return remote(part, part, yl_s.at[d, 2], yl_r.at[d, 2], at_y(far))

    def y_share_last(d):
        part = l_in.at[d, p, :, quarter(y + 2)]
        return remote(part, part, yl_s.at[d, 2], yl_r.at[d, 2], at_y(far))

    def share_x(d):
        get_code_once()
        sort_blocks(d)
        for dx in (2, 1, 3):
            x_share(d, dx).start()

    def share_y(d):
        for dx in (1, 3, 2):
            x_share(d, dx).wait_recv()
        y_share(d, 0).start()
        y_share(d, 1).start()

    def share_pass(d):
        y_share_in(d, p).wait_recv()
        y_share_hop(d).start()

    def swap_blocks(*ds):
        for d in ds:
            if d in SHARED:
                y_share_in(d, 1 - p).wait_recv()
                y_share_last(d).wait_recv()
            else:
                x_block(d, 0).wait_recv()
                x_block(d, 1).wait_recv()
                x_hop(d).wait_recv()
            pair_block(d).start()

    def build_blocks(*ds):
        for d in ds:
            pltpu.make_async_remote_copy(
                src_ref=l_in.at[d, 1 - p], dst_ref=l_in.at[d, 1 - p], send_sem=pl_s.at[d],
                recv_sem=pl_r.at[d], device_id=mate, device_id_type=MESH).wait_recv()
            for k in range(NX):
                for t in range(2):
                    row = d * 4 + t * 2
                    if k == 0:
                        block = l_own[d, t, 0]
                        m0 = meta_own[0, row:row + 1, :]
                        m1 = meta_own[0, row + 1:row + 2, :]
                    else:
                        block = l_in[d, t, k - 1]
                        m0 = meta_in[k - 1, row:row + 1, :]
                        m1 = meta_in[k - 1, row + 1:row + 2, :]
                    cols = slice(t * TILE, (t + 1) * TILE)
                    l_dense[d, k * 256:k * 256 + 128, cols] = block * m0.astype(BF16)
                    l_dense[d, k * 256 + 128:k * 256 + 256, cols] = block * m1.astype(BF16)

    def product(c, d):
        total = jnp.dot(s_all[0, crow(c), :], l_dense[d, 0:256, :], preferred_element_type=F32)
        for k in range(1, NX):
            total += jnp.dot(s_all[k, crow(c), :], l_dense[d, k * 256:(k + 1) * 256, :],
                             preferred_element_type=F32)
        return total

    def z_rows(h, c):
        size = CH // 2 if h == 0 else CH
        return pl.ds(pl.multiple_of(c * size, size), size)

    def z_copy(way, h, c):
        rows = z_rows(h, c)
        return remote(zs.at[way, h, rows], zr.at[way, h, rows], z_s.at[way, h, c], z_r.at[way, h, c],
                      at_z(1 if way == 0 else NZ - 1))

    def z_step(h, c):
        if h == 0:
            x_sum(c, 1 - p).wait_recv()
            x_sum_hop(c).wait_recv()
            total = product(c, 4)
            for way in range(2):
                zs[way, 0, z_rows(0, c), :] = total[way * (CH // 2):(way + 1) * (CH // 2)].astype(BF16)
                z_copy(way, 0, c).start()
            return
        for way in range(2):
            total = product(c, 4 - h if way == 0 else 4 + h)
            z_copy(way, h - 1, c).wait_recv()
            got = zr[way, h - 1, z_rows(h - 1, c), :].astype(F32)
            if h == 1:
                cut = CH // 2
                lo = pl.ds(c * CH, cut)
                hi = pl.ds(c * CH + cut, cut)
                if way == 0:
                    zs[way, h, lo, :] = (total[:cut] + got).astype(BF16)
                    zs[way, h, hi, :] = total[cut:].astype(BF16)
                else:
                    zs[way, h, lo, :] = total[:cut].astype(BF16)
                    zs[way, h, hi, :] = (total[cut:] + got).astype(BF16)
            else:
                zs[way, h, crow(c), :] = (total + got).astype(BF16)
            z_copy(way, h, c).start()

    def pair_out(c):
        rows = pl.ds(pl.multiple_of(p * HALF + c * CH, CH), CH)
        return remote(out.at[0, rows], out.at[0, rows], po_s.at[c], po_r.at[c], mate)

    pair_hole = remote(
        acc.at[pl.ds(pl.multiple_of((1 - p) * HALF, HALF), HALF)], hx, ph_s, ph_r, mate)

    def meta_send():
        get_code_once()
        lax.fori_loop(0, NT, sort_meta, 0, unroll=4)
        x_meta_two().start()
        x_meta(0).start()
        x_meta(1).start()

    def meta_wait():
        x_meta_two().wait_recv()
        x_meta(0).wait_recv()
        x_meta(1).wait_recv()

    def amp_send(j):
        y_amp(j, 0).start()
        y_amp(j, 1).start()

    def amp_pass(j):
        y_amp(j, p).wait_recv()
        y_hop(j).start()

    def block_send(d):
        get_code_once()
        sort_blocks(d)
        send_blocks(d)

    def block_build(d):
        if "meta" not in ready:
            ready.add("meta")
            meta_wait()
        build_blocks(d)

    def hole_part(k):
        if "h" not in ready:
            ready.add("h")
            for g in get_h:
                g.wait()
        if k == 0:
            hole(0, amp_v, "acc" not in ready)
        elif k == 1:
            hole(3 - 2 * p, a_all.at[2 - 2 * p], "acc" not in ready)
        elif k == 2:
            for j in range(NP):
                y_amp(j, 1 - p).wait_recv()
            hole(1 + 2 * p, a_all.at[2 * p], "acc" not in ready)
        else:
            for j in range(NP):
                y_hop(j).wait_recv()
            hole(2, a_all.at[1], "acc" not in ready)
        ready.add("acc")

    def own():
        for c in range(NC):
            fin[crow(c), :] = product(c, 0)

    def finish(c):
        if "hx" not in ready:
            ready.add("hx")
            pair_hole.wait_recv()
        z_copy(0, 3, c).wait_recv()
        z_copy(1, 3, c).wait_recv()
        rows = pl.ds(pl.multiple_of(p * HALF + c * CH, CH), CH)
        total = fin[crow(c), :] + acc[rows, :] + hx[crow(c), :]
        total += zr[0, 3, crow(c), :].astype(F32) + zr[1, 3, crow(c), :].astype(F32)
        out[0, rows, :] = total.astype(BF16)
        pair_out(c).start()

    ready = set()

    def get_code_once():
        if "code" not in ready:
            ready.add("code")
            get_code.wait()
            get_lraw.wait()

    steps = {
        "META": meta_send, "YS": amp_send, "YP": amp_pass, "LS": block_send, "LH": hop_blocks,
        "LX": share_x, "LY": share_y, "LZ": share_pass, "LP": swap_blocks, "LB": block_build, "SS": send_sum, "SH": hop_sum, "Z": z_step,
        "HO": hole_part, "PH": pair_hole.start, "OP": own, "FIN": finish,
    }
    for c in range(NC):
        pair_amp(c).start()
    for g in get_h:
        g.start()
    get_amp.wait()
    for step in PLAN:
        steps[step[0]](*step[1:])

    pair_hole.wait_send()
    for i in range(2):
        x_meta(i).wait_send()
    for j in range(NP):
        y_amp(j, 0).wait_send()
        y_amp(j, 1).wait_send()
        y_hop(j).wait_send()
    x_meta_two().wait_send()

    for d in range(NZ):
        pair_block(d).wait_send()
        if d in SHARED:
            for dx in (1, 2, 3):
                x_share(d, dx).wait_send()
            y_share(d, 0).wait_send()
            y_share(d, 1).wait_send()
            y_share_hop(d).wait_send()
            continue
        x_block(d, 0).wait_send()
        x_block(d, 1).wait_send()
        if d not in DIRECT:
            x_via(d).wait_send()
        x_hop(d).wait_send()

    def drain_c(c, carry):
        pair_amp(c).wait_send()
        x_sum(c, 0).wait_send()
        x_sum(c, 1).wait_send()
        x_sum_hop(c).wait_send()
        for way in range(2):
            for h in range(4):
                z_copy(way, h, c).wait_send()
        pair_out(c).wait_send()
        other = pl.ds(pl.multiple_of((1 - p) * HALF + c * CH, CH), CH)
        remote(out.at[0, other], out.at[0, other], po_s.at[c], po_r.at[c], mate).wait_recv()
        return carry

    lax.fori_loop(0, NC, drain_c, 0)


def on_device(amplitudes, hh_integrals, ladder_blocks, block_target, block_live):
    dma = pltpu.SemaphoreType.DMA
    any_space = pl.BlockSpec(memory_space=pl.ANY)
    vmem = pl.BlockSpec(memory_space=pltpu.VMEM)
    return pl.pallas_call(
        kernel,
        out_shape=pltpu.VMEM((1, ROWS, COLS), BF16),
        in_specs=[any_space] * 5,
        out_specs=vmem,
        scratch_shapes=[
            pltpu.VMEM((ROWS, COLS), BF16),
            pltpu.VMEM((HALF, COLS), BF16),
            pltpu.VMEM((NX, HALF, COLS), BF16),
            pltpu.VMEM((NY - 1, ROWS, COLS), BF16),
            pltpu.VMEM((NY, ROWS, ROWS), BF16),
            pltpu.VMEM((NT, TILE, TILE), BF16),
            pltpu.VMEM((NZ, 2, NX, TILE, TILE), BF16),
            pltpu.VMEM((NZ, 2, NX - 1, TILE, TILE), BF16),
            pltpu.VMEM((NZ, TILE, TILE), BF16),
            pltpu.VMEM((NX, 4 * NZ, TILE), F32),
            pltpu.VMEM((NX - 1, 4 * NZ, TILE), F32),
            pltpu.VMEM((1, NT), jnp.int32),
            pltpu.VMEM((1, NT), jnp.int32),
            pltpu.VMEM((NT, TILE), jnp.int32),
            pltpu.SMEM((NT, TILE), jnp.int32),
            pltpu.VMEM((NZ, NX * COLS, COLS), BF16),
            pltpu.VMEM((2, 4, HALF, COLS), BF16),
            pltpu.VMEM((2, 4, HALF, COLS), BF16),
            pltpu.VMEM((ROWS, COLS), F32),
            pltpu.VMEM((HALF, COLS), F32),
            pltpu.VMEM((HALF, COLS), F32),
            dma, dma, dma, dma, dma, dma((NY,)),
            dma((NC,)), dma((NC,)),
            dma((NP, 3)), dma((NP, 3)),
            dma((NC, 3)), dma((NC, 3)),
            dma((NZ, 4)), dma((NZ, 4)),
            dma((NZ, 3)), dma((NZ, 3)),
            dma((3,)), dma((3,)),
            dma((NZ,)), dma((NZ,)),
            dma((2, 4, NC)), dma((2, 4, NC)),
            dma, dma,
            dma((NC,)), dma((NC,)),
        ],
        compiler_params=pltpu.CompilerParams(
            collective_id=0, has_side_effects=True, vmem_limit_bytes=56 * 2**20),
        cost_estimate=pl.CostEstimate(
            flops=4 * ROWS * 4096 * COLS, bytes_accessed=12 * 2**20, transcendentals=0),
        name="ladder_hole",
    )(block_target, block_live, amplitudes, hh_integrals, ladder_blocks)


def solution(mesh):
    return jax.shard_map(
        on_device,
        mesh=mesh,
        in_specs=(
            P("pair", "occ", "vir"),
            P("pair", "occ", None),
            P("vir", None, None, None),
            P("vir", None),
            P("vir", None),
        ),
        out_specs=P("pair", "occ", "vir"),
        check_vma=False,
    )
```

```python
import jax
import jax.numpy as jnp
from jax import lax
from jax.experimental import pallas as pl
from jax.experimental.pallas import tpu as pltpu
from jax.sharding import PartitionSpec as P

MESH = pl.DeviceIdType.MESH
TILE = 128
NX = 4
NY = 4
NZ = 8
NT = 64
ROWS = 1024
HALF = 512
COLS = 256
CH = 128
NC = HALF // CH
NP = 4
PIECE = ROWS // NP
DIRECT = ()
SHARED = (4, 3, 5)

PLAN = (
    ("YS", 1), ("LX", 4), ("LX", 5), ("LX", 3), ("SS", 3), ("SS", 0), ("LY", 4), ("LY", 5), ("LY", 3),
    ("SS", 2), ("SS", 1), ("META",), ("LZ", 4), ("LZ", 5), ("SH", 3), ("HO", 0), ("SH", 0), ("LZ", 3),
    ("SH", 2), ("YS", 0), ("LP", 4), ("LP", 5), ("SH", 1), ("LB", 4), ("LS", 6), ("YP", 1), ("YS", 2),
    ("LS", 2), ("Z", 0, 3), ("Z", 0, 0), ("LP", 3), ("Z", 0, 2), ("LS", 7), ("YS", 3), ("Z", 0, 1),
    ("LB", 3), ("LH", 6), ("LB", 5), ("Z", 1, 3), ("LH", 2), ("Z", 1, 2), ("LS", 1), ("Z", 1, 0), ("YP", 0),
    ("LH", 7), ("LP", 6), ("Z", 1, 1), ("LP", 2), ("LH", 1), ("LB", 6), ("LB", 2), ("YP", 2), ("Z", 2, 3),
    ("Z", 2, 2), ("LS", 0), ("LP", 7), ("Z", 2, 0), ("YP", 3), ("LB", 7), ("HO", 2), ("HO", 1), ("LH", 0),
    ("LP", 1), ("Z", 2, 1), ("LB", 1), ("Z", 3, 3), ("LP", 0), ("Z", 3, 0), ("LB", 0), ("Z", 3, 2), ("OP",),
    ("Z", 3, 1), ("HO", 3), ("PH",), ("FIN", 2), ("FIN", 0), ("FIN", 3), ("FIN", 1),
)
F32 = jnp.float32
BF16 = jnp.bfloat16


def kernel(target, live, amp, hh, blocks, out,
           amp_v, aoth, s_all, a_all, h_v, l_raw, l_own, l_in, l_via, meta_own, meta_in, target_v, live_v, code_v, code,
           l_dense, zs, zr, acc, hx, fin,
           sem_target, sem_live, sem_lraw, sem_amp, sem_code, sem_h, pa_s, pa_r, ya_s, ya_r, xs_s, xs_r, xl_s, xl_r, yl_s, yl_r,
           xm_s, xm_r, pl_s, pl_r, z_s, z_r, ph_s, ph_r, po_s, po_r):
    y = lax.axis_index("occ")
    v = lax.axis_index("vir")
    p = lax.axis_index("pair")
    z = v // NX
    x = v % NX
    far = 1 + 2 * p

    def at_x(dx):
        return {"occ": y, "vir": z * NX + (x + dx) % NX, "pair": p}

    def at_y(dy):
        return {"occ": (y + dy) % NY, "vir": v, "pair": p}

    def at_z(dz):
        return {"occ": y, "vir": ((z + dz) % NZ) * NX + x, "pair": p}

    mate = {"occ": y, "vir": v, "pair": 1 - p}

    def remote(src, dst, ss, rs, dev):
        return pltpu.make_async_remote_copy(
            src_ref=src, dst_ref=dst, send_sem=ss, recv_sem=rs,
            device_id=dev, device_id_type=MESH)

    def crow(c):
        return pl.ds(pl.multiple_of(c * CH, CH), CH)

    barrier = pltpu.get_barrier_semaphore()
    peers = [at_x(1), at_x(2), at_x(3), at_y(1), at_y(3), at_z(1), at_z(NZ - 1), mate]
    for dev in peers:
        pl.semaphore_signal(barrier, inc=1, device_id=dev, device_id_type=MESH)

    get_lraw = pltpu.make_async_copy(blocks.at[0], l_raw, sem_lraw)
    get_amp = pltpu.make_async_copy(amp.at[0], amp_v, sem_amp)
    get_h = [
        pltpu.make_async_copy(
            hh.at[0, :, pl.ds(pl.multiple_of(((y + k) % NY) * ROWS, ROWS), ROWS)],
            h_v.at[k], sem_h.at[k])
        for k in range(NY)
    ]
    get_target = pltpu.make_async_copy(target, target_v, sem_target)
    get_live = pltpu.make_async_copy(live, live_v, sem_live)
    get_target.start()
    get_live.start()
    get_lraw.start()
    get_amp.start()
    get_target.wait()
    get_live.wait()

    entry = lax.broadcasted_iota(jnp.int32, (NT, NT), 1)
    hit = jnp.broadcast_to(target_v[...], (NT, NT)) == lax.broadcasted_iota(jnp.int32, (NT, NT), 0)
    value = 2 * entry + jnp.broadcast_to(live_v[...], (NT, NT))
    found = jnp.max(jnp.where(hit, value, 0), axis=1, keepdims=True)
    code_v[...] = jnp.broadcast_to(found, (NT, TILE))
    get_code = pltpu.make_async_copy(code_v, code, sem_code)
    get_code.start()

    def sort_blocks(*ds):
        for d in ds:
            for t in range(2):
                for dx in range(NX):
                    tile = 2 * (((z + d) % NZ) * NX + (x + dx) % NX) + t
                    l_own[d, t, dx] = l_raw[code[tile, 0] // 2]

    def sort_meta(i, carry):
        d = i // 8
        t = (i // 4) % 2
        dx = i % 4
        tile = 2 * (((z + d) % NZ) * NX + (x + dx) % NX) + t
        both = code[tile, 0]
        alive = (both % 2).astype(F32)
        upper = jnp.where(both < NT, alive, 0.0)
        row = d * 4 + t * 2
        meta_own[dx, pl.ds(row, 1), :] = jnp.full((1, TILE), upper, F32)
        meta_own[dx, pl.ds(row + 1, 1), :] = jnp.full((1, TILE), alive - upper, F32)
        return carry

    pl.semaphore_wait(barrier, len(peers))

    def pair_amp(c):
        return remote(
            amp.at[0, pl.ds(pl.multiple_of((1 - p) * HALF + c * CH, CH), CH)],
            aoth.at[crow(c)], pa_s.at[c], pa_r.at[c], mate)

    def y_amp(j, i):
        rows = pl.ds(j * PIECE, PIECE)
        return remote(amp.at[0, rows], a_all.at[2 - 2 * i, rows], ya_s.at[j, i], ya_r.at[j, i], at_y(1 + 2 * i))

    def y_hop(j):
        rows = pl.ds(j * PIECE, PIECE)
        return remote(a_all.at[2 - 2 * p, rows], a_all.at[1, rows], ya_s.at[j, 2], ya_r.at[j, 2], at_y(far))

    def x_meta(i):
        return remote(meta_own.at[1 + 2 * i], meta_in.at[2 - 2 * i], xm_s.at[i], xm_r.at[i], at_x(1 + 2 * i))

    def x_meta_two():
        return remote(meta_own.at[2], meta_in.at[1], xm_s.at[2], xm_r.at[2], at_x(2))

    def x_block(d, i):
        return remote(l_own.at[d, p, 1 + 2 * i], l_in.at[d, p, 2 - 2 * i],
                      xl_s.at[d, i], xl_r.at[d, i], at_x(1 + 2 * i))

    def x_via(d):
        return remote(l_own.at[d, p, 2], l_via.at[d], xl_s.at[d, 2], xl_r.at[d, 2], at_x(far))

    def x_two(d):
        return remote(l_own.at[d, p, 2], l_in.at[d, p, 1], xl_s.at[d, 3], xl_r.at[d, 3], at_x(2))

    def x_hop(d):
        if d in DIRECT:
            return x_two(d)
        return remote(l_via.at[d], l_in.at[d, p, 1], xl_s.at[d, 3], xl_r.at[d, 3], at_x(far))

    def x_sum(c, i):
        return remote(s_all.at[0, crow(c)], s_all.at[3 - 2 * i, crow(c)],
                      xs_s.at[c, i], xs_r.at[c, i], at_x(1 + 2 * i))

    def x_sum_hop(c):
        return remote(s_all.at[3 - 2 * p, crow(c)], s_all.at[2, crow(c)],
                      xs_s.at[c, 2], xs_r.at[c, 2], at_x(far))

    def pair_block(d):
        return remote(l_in.at[d, p], l_in.at[d, p], pl_s.at[d], pl_r.at[d], mate)

    def send_blocks(*ds):
        for d in ds:
            if d in DIRECT:
                x_two(d).start()
            else:
                x_via(d).start()
            x_block(d, 0).start()
            x_block(d, 1).start()

    def hop_blocks(*ds):
        for d in ds:
            x_via(d).wait_recv()
            x_hop(d).start()

    def send_sum(c):
        pair_amp(c).wait_recv()
        mine = amp_v[pl.ds(pl.multiple_of(p * HALF + c * CH, CH), CH), :]
        s_all[0, crow(c), :] = (mine.astype(F32) + aoth[crow(c), :].astype(F32)).astype(BF16)
        x_sum(c, 0).start()
        x_sum(c, 1).start()

    def hop_sum(c):
        x_sum(c, p).wait_recv()
        x_sum_hop(c).start()

    def hole(k, a_ref, first):
        def step(i, carry):
            rows = pl.ds(pl.multiple_of(i * 256, 256), 256)
            term = jnp.dot(h_v[k, rows, :], a_ref[...], preferred_element_type=F32)
            if first:
                acc[rows, :] = term
            else:
                acc[rows, :] += term
            return carry
        lax.fori_loop(0, ROWS // 256, step, 0)

    def quarter(q):
        return pl.ds(pl.multiple_of((q % NY) * 32, 32), 32)

    def x_share(d, dx):
        return remote(l_own.at[d, p, dx, quarter(y)], l_in.at[d, p, NX - dx - 1, quarter(y)],
                      xl_s.at[d, dx - 1], xl_r.at[d, NX - dx - 1], at_x(dx))

    def y_share(d, i):
        return remote(l_in.at[d, p, :, quarter(y)], l_in.at[d, p, :, quarter(y)],
                      yl_s.at[d, i], yl_r.at[d, i], at_y(1 + 2 * i))

    def y_share_in(d, i):
        part = l_in.at[d, p, :, quarter(y + 3 - 2 * i)]
        return remote(part, part, yl_s.at[d, i], yl_r.at[d, i], at_y(1 + 2 * i))

    def y_share_hop(d):
        part = l_in.at[d, p, :, quarter(y + 3 - 2 * p)]
        return remote(part, part, yl_s.at[d, 2], yl_r.at[d, 2], at_y(far))

    def y_share_last(d):
        part = l_in.at[d, p, :, quarter(y + 2)]
        return remote(part, part, yl_s.at[d, 2], yl_r.at[d, 2], at_y(far))

    def share_x(d):
        get_code_once()
        sort_blocks(d)
        for dx in (2, 1, 3):
            x_share(d, dx).start()

    def share_y(d):
        for dx in (1, 3, 2):
            x_share(d, dx).wait_recv()
        y_share(d, 0).start()
        y_share(d, 1).start()

    def share_pass(d):
        y_share_in(d, p).wait_recv()
        y_share_hop(d).start()

    def swap_blocks(*ds):
        for d in ds:
            if d in SHARED:
                y_share_in(d, 1 - p).wait_recv()
                y_share_last(d).wait_recv()
            else:
                x_block(d, 0).wait_recv()
                x_block(d, 1).wait_recv()
                x_hop(d).wait_recv()
            pair_block(d).start()

    def build_blocks(*ds):
        for d in ds:
            pltpu.make_async_remote_copy(
                src_ref=l_in.at[d, 1 - p], dst_ref=l_in.at[d, 1 - p], send_sem=pl_s.at[d],
                recv_sem=pl_r.at[d], device_id=mate, device_id_type=MESH).wait_recv()
            for k in range(NX):
                for t in range(2):
                    row = d * 4 + t * 2
                    if k == 0:
                        block = l_own[d, t, 0]
                        m0 = meta_own[0, row:row + 1, :]
                        m1 = meta_own[0, row + 1:row + 2, :]
                    else:
                        block = l_in[d, t, k - 1]
                        m0 = meta_in[k - 1, row:row + 1, :]
                        m1 = meta_in[k - 1, row + 1:row + 2, :]
                    cols = slice(t * TILE, (t + 1) * TILE)
                    l_dense[d, k * 256:k * 256 + 128, cols] = block * m0.astype(BF16)
                    l_dense[d, k * 256 + 128:k * 256 + 256, cols] = block * m1.astype(BF16)

    def product(c, d):
        total = jnp.dot(s_all[0, crow(c), :], l_dense[d, 0:256, :], preferred_element_type=F32)
        for k in range(1, NX):
            total += jnp.dot(s_all[k, crow(c), :], l_dense[d, k * 256:(k + 1) * 256, :],
                             preferred_element_type=F32)
        return total

    def z_rows(h, c):
        size = CH // 2 if h == 0 else CH
        return pl.ds(pl.multiple_of(c * size, size), size)

    def z_copy(way, h, c):
        rows = z_rows(h, c)
        return remote(zs.at[way, h, rows], zr.at[way, h, rows], z_s.at[way, h, c], z_r.at[way, h, c],
                      at_z(1 if way == 0 else NZ - 1))

    def z_step(h, c):
        if h == 0:
            x_sum(c, 1 - p).wait_recv()
            x_sum_hop(c).wait_recv()
            total = product(c, 4)
            for way in range(2):
                zs[way, 0, z_rows(0, c), :] = total[way * (CH // 2):(way + 1) * (CH // 2)].astype(BF16)
                z_copy(way, 0, c).start()
            return
        for way in range(2):
            total = product(c, 4 - h if way == 0 else 4 + h)
            z_copy(way, h - 1, c).wait_recv()
            got = zr[way, h - 1, z_rows(h - 1, c), :].astype(F32)
            if h == 1:
                cut = CH // 2
                lo = pl.ds(c * CH, cut)
                hi = pl.ds(c * CH + cut, cut)
                if way == 0:
                    zs[way, h, lo, :] = (total[:cut] + got).astype(BF16)
                    zs[way, h, hi, :] = total[cut:].astype(BF16)
                else:
                    zs[way, h, lo, :] = total[:cut].astype(BF16)
                    zs[way, h, hi, :] = (total[cut:] + got).astype(BF16)
            else:
                zs[way, h, crow(c), :] = (total + got).astype(BF16)
            z_copy(way, h, c).start()

    def pair_out(c):
        rows = pl.ds(pl.multiple_of(p * HALF + c * CH, CH), CH)
        return remote(out.at[0, rows], out.at[0, rows], po_s.at[c], po_r.at[c], mate)

    pair_hole = remote(
        acc.at[pl.ds(pl.multiple_of((1 - p) * HALF, HALF), HALF)], hx, ph_s, ph_r, mate)

    def meta_send():
        get_code_once()
        lax.fori_loop(0, NT, sort_meta, 0, unroll=4)
        x_meta_two().start()
        x_meta(0).start()
        x_meta(1).start()

    def meta_wait():
        x_meta_two().wait_recv()
        x_meta(0).wait_recv()
        x_meta(1).wait_recv()

    def amp_send(j):
        y_amp(j, 0).start()
        y_amp(j, 1).start()

    def amp_pass(j):
        y_amp(j, p).wait_recv()
        y_hop(j).start()

    def block_send(d):
        get_code_once()
        sort_blocks(d)
        send_blocks(d)

    def block_build(d):
        if "meta" not in ready:
            ready.add("meta")
            meta_wait()
        build_blocks(d)

    def hole_part(k):
        if "h" not in ready:
            ready.add("h")
            for g in get_h:
                g.wait()
        if k == 0:
            hole(0, amp_v, "acc" not in ready)
        elif k == 1:
            hole(3 - 2 * p, a_all.at[2 - 2 * p], "acc" not in ready)
        elif k == 2:
            for j in range(NP):
                y_amp(j, 1 - p).wait_recv()
            hole(1 + 2 * p, a_all.at[2 * p], "acc" not in ready)
        else:
            for j in range(NP):
                y_hop(j).wait_recv()
            hole(2, a_all.at[1], "acc" not in ready)
        ready.add("acc")

    def own():
        for c in range(NC):
            fin[crow(c), :] = product(c, 0)

    def finish(c):
        if "hx" not in ready:
            ready.add("hx")
            pair_hole.wait_recv()
        z_copy(0, 3, c).wait_recv()
        z_copy(1, 3, c).wait_recv()
        rows = pl.ds(pl.multiple_of(p * HALF + c * CH, CH), CH)
        total = fin[crow(c), :] + acc[rows, :] + hx[crow(c), :]
        total += zr[0, 3, crow(c), :].astype(F32) + zr[1, 3, crow(c), :].astype(F32)
        out[0, rows, :] = total.astype(BF16)
        pair_out(c).start()

    ready = set()

    def get_code_once():
        if "code" not in ready:
            ready.add("code")
            get_code.wait()
            get_lraw.wait()

    steps = {
        "META": meta_send, "YS": amp_send, "YP": amp_pass, "LS": block_send, "LH": hop_blocks,
        "LX": share_x, "LY": share_y, "LZ": share_pass, "LP": swap_blocks, "LB": block_build, "SS": send_sum, "SH": hop_sum, "Z": z_step,
        "HO": hole_part, "PH": pair_hole.start, "OP": own, "FIN": finish,
    }
    for c in range(NC):
        pair_amp(c).start()
    for g in get_h:
        g.start()
    get_amp.wait()
    for step in PLAN:
        steps[step[0]](*step[1:])

    pair_hole.wait_send()
    for i in range(2):
        x_meta(i).wait_send()
    for j in range(NP):
        y_amp(j, 0).wait_send()
        y_amp(j, 1).wait_send()
        y_hop(j).wait_send()
    x_meta_two().wait_send()

    for d in range(NZ):
        pair_block(d).wait_send()
        if d in SHARED:
            for dx in (1, 2, 3):
                x_share(d, dx).wait_send()
            y_share(d, 0).wait_send()
            y_share(d, 1).wait_send()
            y_share_hop(d).wait_send()
            continue
        x_block(d, 0).wait_send()
        x_block(d, 1).wait_send()
        if d not in DIRECT:
            x_via(d).wait_send()
        x_hop(d).wait_send()

    def drain_c(c, carry):
        pair_amp(c).wait_send()
        x_sum(c, 0).wait_send()
        x_sum(c, 1).wait_send()
        x_sum_hop(c).wait_send()
        for way in range(2):
            for h in range(4):
                z_copy(way, h, c).wait_send()
        pair_out(c).wait_send()
        other = pl.ds(pl.multiple_of((1 - p) * HALF + c * CH, CH), CH)
        remote(out.at[0, other], out.at[0, other], po_s.at[c], po_r.at[c], mate).wait_recv()
        return carry

    lax.fori_loop(0, NC, drain_c, 0)


def on_device(amplitudes, hh_integrals, ladder_blocks, block_target, block_live):
    dma = pltpu.SemaphoreType.DMA
    any_space = pl.BlockSpec(memory_space=pl.ANY)
    vmem = pl.BlockSpec(memory_space=pltpu.VMEM)
    return pl.pallas_call(
        kernel,
        out_shape=pltpu.VMEM((1, ROWS, COLS), BF16),
        in_specs=[any_space] * 5,
        out_specs=vmem,
        scratch_shapes=[
            pltpu.VMEM((ROWS, COLS), BF16),
            pltpu.VMEM((HALF, COLS), BF16),
            pltpu.VMEM((NX, HALF, COLS), BF16),
            pltpu.VMEM((NY - 1, ROWS, COLS), BF16),
            pltpu.VMEM((NY, ROWS, ROWS), BF16),
            pltpu.VMEM((NT, TILE, TILE), BF16),
            pltpu.VMEM((NZ, 2, NX, TILE, TILE), BF16),
            pltpu.VMEM((NZ, 2, NX - 1, TILE, TILE), BF16),
            pltpu.VMEM((NZ, TILE, TILE), BF16),
            pltpu.VMEM((NX, 4 * NZ, TILE), F32),
            pltpu.VMEM((NX - 1, 4 * NZ, TILE), F32),
            pltpu.VMEM((1, NT), jnp.int32),
            pltpu.VMEM((1, NT), jnp.int32),
            pltpu.VMEM((NT, TILE), jnp.int32),
            pltpu.SMEM((NT, TILE), jnp.int32),
            pltpu.VMEM((NZ, NX * COLS, COLS), BF16),
            pltpu.VMEM((2, 4, HALF, COLS), BF16),
            pltpu.VMEM((2, 4, HALF, COLS), BF16),
            pltpu.VMEM((ROWS, COLS), F32),
            pltpu.VMEM((HALF, COLS), F32),
            pltpu.VMEM((HALF, COLS), F32),
            dma, dma, dma, dma, dma, dma((NY,)),
            dma((NC,)), dma((NC,)),
            dma((NP, 3)), dma((NP, 3)),
            dma((NC, 3)), dma((NC, 3)),
            dma((NZ, 4)), dma((NZ, 4)),
            dma((NZ, 3)), dma((NZ, 3)),
            dma((3,)), dma((3,)),
            dma((NZ,)), dma((NZ,)),
            dma((2, 4, NC)), dma((2, 4, NC)),
            dma, dma,
            dma((NC,)), dma((NC,)),
        ],
        compiler_params=pltpu.CompilerParams(
            collective_id=0, has_side_effects=True, vmem_limit_bytes=56 * 2**20),
        cost_estimate=pl.CostEstimate(
            flops=4 * ROWS * 4096 * COLS, bytes_accessed=12 * 2**20, transcendentals=0),
        name="ladder_hole",
    )(block_target, block_live, amplitudes, hh_integrals, ladder_blocks)


def solution(mesh):
    return jax.shard_map(
        on_device,
        mesh=mesh,
        in_specs=(
            P("pair", "occ", "vir"),
            P("pair", "occ", None),
            P("vir", None, None, None),
            P("vir", None),
            P("vir", None),
        ),
        out_specs=P("pair", "occ", "vir"),
        check_vma=False,
    )
```

```python
import jax
import jax.numpy as jnp
from jax import lax
from jax.experimental import pallas as pl
from jax.experimental.pallas import tpu as pltpu
from jax.sharding import PartitionSpec as P

MESH = pl.DeviceIdType.MESH
TILE = 128
NX = 4
NY = 4
NZ = 8
NT = 64
ROWS = 1024
HALF = 512
COLS = 256
CH = 128
NC = HALF // CH
NP = 4
PIECE = ROWS // NP
DIRECT = ()
SHARED = (4, 3, 5)

PLAN = (
    ("LX", 4), ("LX", 3), ("YS", 3), ("LX", 5), ("SS", 0), ("LY", 4), ("SS", 3), ("LY", 3), ("SS", 1),
    ("SS", 2), ("LY", 5), ("META",), ("LZ", 4), ("LZ", 3), ("LZ", 5), ("SH", 0), ("YS", 2), ("SH", 1),
    ("LP", 4), ("SH", 3), ("LP", 3), ("SH", 2), ("LP", 5), ("LS", 2), ("LB", 4), ("Z", 0, 0), ("LS", 6),
    ("YS", 1), ("LS", 1), ("Z", 0, 1), ("YS", 0), ("Z", 0, 3), ("Z", 0, 2), ("LB", 5), ("LB", 3), ("YP", 2),
    ("Z", 1, 0), ("LH", 6), ("YP", 3), ("LH", 2), ("LS", 7), ("Z", 1, 3), ("Z", 1, 2), ("LH", 1),
    ("Z", 1, 1), ("LP", 6), ("LP", 2), ("LH", 7), ("YP", 1), ("LS", 0), ("LB", 6), ("LP", 1), ("YP", 0),
    ("LB", 2), ("Z", 2, 0), ("LP", 7), ("Z", 2, 2), ("LH", 0), ("Z", 2, 3), ("Z", 2, 1), ("LB", 1),
    ("LP", 0), ("LB", 7), ("Z", 3, 2), ("LB", 0), ("Z", 3, 0), ("HO", 3), ("HO", 2), ("OP",), ("Z", 3, 1),
    ("HO", 1), ("HO", 0), ("Z", 3, 3), ("PH",), ("FIN", 1), ("FIN", 2), ("FIN", 0), ("FIN", 3),
)
F32 = jnp.float32
BF16 = jnp.bfloat16


def kernel(target, live, amp, hh, blocks, out,
           amp_v, aoth, s_all, a_all, h_v, l_raw, l_own, l_in, l_via, meta_own, meta_in, target_v, live_v, code_v, code,
           l_dense, zs, zr, acc, hx, fin,
           sem_target, sem_live, sem_lraw, sem_amp, sem_code, sem_h, pa_s, pa_r, ya_s, ya_r, xs_s, xs_r, xl_s, xl_r, yl_s, yl_r,
           xm_s, xm_r, pl_s, pl_r, z_s, z_r, ph_s, ph_r, po_s, po_r):
    y = lax.axis_index("occ")
    v = lax.axis_index("vir")
    p = lax.axis_index("pair")
    z = v // NX
    x = v % NX
    far = 1 + 2 * p

    def at_x(dx):
        return {"occ": y, "vir": z * NX + (x + dx) % NX, "pair": p}

    def at_y(dy):
        return {"occ": (y + dy) % NY, "vir": v, "pair": p}

    def at_z(dz):
        return {"occ": y, "vir": ((z + dz) % NZ) * NX + x, "pair": p}

    mate = {"occ": y, "vir": v, "pair": 1 - p}

    def remote(src, dst, ss, rs, dev):
        return pltpu.make_async_remote_copy(
            src_ref=src, dst_ref=dst, send_sem=ss, recv_sem=rs,
            device_id=dev, device_id_type=MESH)

    def crow(c):
        return pl.ds(pl.multiple_of(c * CH, CH), CH)

    barrier = pltpu.get_barrier_semaphore()
    peers = [at_x(1), at_x(2), at_x(3), at_y(1), at_y(3), at_z(1), at_z(NZ - 1), mate]
    for dev in peers:
        pl.semaphore_signal(barrier, inc=1, device_id=dev, device_id_type=MESH)

    get_lraw = pltpu.make_async_copy(blocks.at[0], l_raw, sem_lraw)
    get_amp = pltpu.make_async_copy(amp.at[0], amp_v, sem_amp)
    get_h = [
        pltpu.make_async_copy(
            hh.at[0, :, pl.ds(pl.multiple_of(((y + k) % NY) * ROWS, ROWS), ROWS)],
            h_v.at[k], sem_h.at[k])
        for k in range(NY)
    ]
    get_target = pltpu.make_async_copy(target, target_v, sem_target)
    get_live = pltpu.make_async_copy(live, live_v, sem_live)
    get_target.start()
    get_live.start()
    get_lraw.start()
    get_amp.start()
    get_target.wait()
    get_live.wait()

    entry = lax.broadcasted_iota(jnp.int32, (NT, NT), 1)
    hit = jnp.broadcast_to(target_v[...], (NT, NT)) == lax.broadcasted_iota(jnp.int32, (NT, NT), 0)
    value = 2 * entry + jnp.broadcast_to(live_v[...], (NT, NT))
    found = jnp.max(jnp.where(hit, value, 0), axis=1, keepdims=True)
    code_v[...] = jnp.broadcast_to(found, (NT, TILE))
    get_code = pltpu.make_async_copy(code_v, code, sem_code)
    get_code.start()

    def sort_blocks(*ds):
        for d in ds:
            for t in range(2):
                for dx in range(NX):
                    tile = 2 * (((z + d) % NZ) * NX + (x + dx) % NX) + t
                    l_own[d, t, dx] = l_raw[code[tile, 0] // 2]

    def sort_meta(i, carry):
        d = i // 8
        t = (i // 4) % 2
        dx = i % 4
        tile = 2 * (((z + d) % NZ) * NX + (x + dx) % NX) + t
        both = code[tile, 0]
        alive = (both % 2).astype(F32)
        upper = jnp.where(both < NT, alive, 0.0)
        row = d * 4 + t * 2
        meta_own[dx, pl.ds(row, 1), :] = jnp.full((1, TILE), upper, F32)
        meta_own[dx, pl.ds(row + 1, 1), :] = jnp.full((1, TILE), alive - upper, F32)
        return carry

    pl.semaphore_wait(barrier, len(peers))

    def pair_amp(c):
        return remote(
            amp.at[0, pl.ds(pl.multiple_of((1 - p) * HALF + c * CH, CH), CH)],
            aoth.at[crow(c)], pa_s.at[c], pa_r.at[c], mate)

    def y_amp(j, i):
        rows = pl.ds(j * PIECE, PIECE)
        return remote(amp.at[0, rows], a_all.at[2 - 2 * i, rows], ya_s.at[j, i], ya_r.at[j, i], at_y(1 + 2 * i))

    def y_hop(j):
        rows = pl.ds(j * PIECE, PIECE)
        return remote(a_all.at[2 - 2 * p, rows], a_all.at[1, rows], ya_s.at[j, 2], ya_r.at[j, 2], at_y(far))

    def x_meta(i):
        return remote(meta_own.at[1 + 2 * i], meta_in.at[2 - 2 * i], xm_s.at[i], xm_r.at[i], at_x(1 + 2 * i))

    def x_meta_two():
        return remote(meta_own.at[2], meta_in.at[1], xm_s.at[2], xm_r.at[2], at_x(2))

    def x_block(d, i):
        return remote(l_own.at[d, p, 1 + 2 * i], l_in.at[d, p, 2 - 2 * i],
                      xl_s.at[d, i], xl_r.at[d, i], at_x(1 + 2 * i))

    def x_via(d):
        return remote(l_own.at[d, p, 2], l_via.at[d], xl_s.at[d, 2], xl_r.at[d, 2], at_x(far))

    def x_two(d):
        return remote(l_own.at[d, p, 2], l_in.at[d, p, 1], xl_s.at[d, 3], xl_r.at[d, 3], at_x(2))

    def x_hop(d):
        if d in DIRECT:
            return x_two(d)
        return remote(l_via.at[d], l_in.at[d, p, 1], xl_s.at[d, 3], xl_r.at[d, 3], at_x(far))

    def x_sum(c, i):
        return remote(s_all.at[0, crow(c)], s_all.at[3 - 2 * i, crow(c)],
                      xs_s.at[c, i], xs_r.at[c, i], at_x(1 + 2 * i))

    def x_sum_hop(c):
        return remote(s_all.at[3 - 2 * p, crow(c)], s_all.at[2, crow(c)],
                      xs_s.at[c, 2], xs_r.at[c, 2], at_x(far))

    def pair_block(d):
        return remote(l_in.at[d, p], l_in.at[d, p], pl_s.at[d], pl_r.at[d], mate)

    def send_blocks(*ds):
        for d in ds:
            if d in DIRECT:
                x_two(d).start()
            else:
                x_via(d).start()
            x_block(d, 0).start()
            x_block(d, 1).start()

    def hop_blocks(*ds):
        for d in ds:
            x_via(d).wait_recv()
            x_hop(d).start()

    def send_sum(c):
        pair_amp(c).wait_recv()
        mine = amp_v[pl.ds(pl.multiple_of(p * HALF + c * CH, CH), CH), :]
        s_all[0, crow(c), :] = (mine.astype(F32) + aoth[crow(c), :].astype(F32)).astype(BF16)
        x_sum(c, 0).start()
        x_sum(c, 1).start()

    def hop_sum(c):
        x_sum(c, p).wait_recv()
        x_sum_hop(c).start()

    def hole(k, a_ref, first):
        def step(i, carry):
            rows = pl.ds(pl.multiple_of(i * 256, 256), 256)
            term = jnp.dot(h_v[k, rows, :], a_ref[...], preferred_element_type=F32)
            if first:
                acc[rows, :] = term
            else:
                acc[rows, :] += term
            return carry
        lax.fori_loop(0, ROWS // 256, step, 0)

    def quarter(q):
        return pl.ds(pl.multiple_of((q % NY) * 32, 32), 32)

    def x_share(d, dx):
        return remote(l_own.at[d, p, dx, quarter(y)], l_in.at[d, p, NX - dx - 1, quarter(y)],
                      xl_s.at[d, dx - 1], xl_r.at[d, NX - dx - 1], at_x(dx))

    def y_share(d, i):
        return remote(l_in.at[d, p, :, quarter(y)], l_in.at[d, p, :, quarter(y)],
                      yl_s.at[d, i], yl_r.at[d, i], at_y(1 + 2 * i))

    def y_share_in(d, i):
        part = l_in.at[d, p, :, quarter(y + 3 - 2 * i)]
        return remote(part, part, yl_s.at[d, i], yl_r.at[d, i], at_y(1 + 2 * i))

    def y_share_hop(d):
        part = l_in.at[d, p, :, quarter(y + 3 - 2 * p)]
        return remote(part, part, yl_s.at[d, 2], yl_r.at[d, 2], at_y(far))

    def y_share_last(d):
        part = l_in.at[d, p, :, quarter(y + 2)]
        return remote(part, part, yl_s.at[d, 2], yl_r.at[d, 2], at_y(far))

    def share_x(d):
        get_code_once()
        sort_blocks(d)
        for dx in (2, 1, 3):
            x_share(d, dx).start()

    def share_y(d):
        for dx in (1, 3, 2):
            x_share(d, dx).wait_recv()
        y_share(d, 0).start()
        y_share(d, 1).start()

    def share_pass(d):
        y_share_in(d, p).wait_recv()
        y_share_hop(d).start()

    def swap_blocks(*ds):
        for d in ds:
            if d in SHARED:
                y_share_in(d, 1 - p).wait_recv()
                y_share_last(d).wait_recv()
            else:
                x_block(d, 0).wait_recv()
                x_block(d, 1).wait_recv()
                x_hop(d).wait_recv()
            pair_block(d).start()

    def build_blocks(*ds):
        for d in ds:
            pltpu.make_async_remote_copy(
                src_ref=l_in.at[d, 1 - p], dst_ref=l_in.at[d, 1 - p], send_sem=pl_s.at[d],
                recv_sem=pl_r.at[d], device_id=mate, device_id_type=MESH).wait_recv()
            for k in range(NX):
                for t in range(2):
                    row = d * 4 + t * 2
                    if k == 0:
                        block = l_own[d, t, 0]
                        m0 = meta_own[0, row:row + 1, :]
                        m1 = meta_own[0, row + 1:row + 2, :]
                    else:
                        block = l_in[d, t, k - 1]
                        m0 = meta_in[k - 1, row:row + 1, :]
                        m1 = meta_in[k - 1, row + 1:row + 2, :]
                    cols = slice(t * TILE, (t + 1) * TILE)
                    l_dense[d, k * 256:k * 256 + 128, cols] = block * m0.astype(BF16)
                    l_dense[d, k * 256 + 128:k * 256 + 256, cols] = block * m1.astype(BF16)

    def product(c, d):
        total = jnp.dot(s_all[0, crow(c), :], l_dense[d, 0:256, :], preferred_element_type=F32)
        for k in range(1, NX):
            total += jnp.dot(s_all[k, crow(c), :], l_dense[d, k * 256:(k + 1) * 256, :],
                             preferred_element_type=F32)
        return total

    def z_rows(h, c):
        size = CH // 2 if h == 0 else CH
        return pl.ds(pl.multiple_of(c * size, size), size)

    def z_copy(way, h, c):
        rows = z_rows(h, c)
        return remote(zs.at[way, h, rows], zr.at[way, h, rows], z_s.at[way, h, c], z_r.at[way, h, c],
                      at_z(1 if way == 0 else NZ - 1))

    def z_step(h, c):
        if h == 0:
            x_sum(c, 1 - p).wait_recv()
            x_sum_hop(c).wait_recv()
            total = product(c, 4)
            for way in range(2):
                zs[way, 0, z_rows(0, c), :] = total[way * (CH // 2):(way + 1) * (CH // 2)].astype(BF16)
                z_copy(way, 0, c).start()
            return
        for way in range(2):
            total = product(c, 4 - h if way == 0 else 4 + h)
            z_copy(way, h - 1, c).wait_recv()
            got = zr[way, h - 1, z_rows(h - 1, c), :].astype(F32)
            if h == 1:
                cut = CH // 2
                lo = pl.ds(c * CH, cut)
                hi = pl.ds(c * CH + cut, cut)
                if way == 0:
                    zs[way, h, lo, :] = (total[:cut] + got).astype(BF16)
                    zs[way, h, hi, :] = total[cut:].astype(BF16)
                else:
                    zs[way, h, lo, :] = total[:cut].astype(BF16)
                    zs[way, h, hi, :] = (total[cut:] + got).astype(BF16)
            else:
                zs[way, h, crow(c), :] = (total + got).astype(BF16)
            z_copy(way, h, c).start()

    def pair_out(c):
        rows = pl.ds(pl.multiple_of(p * HALF + c * CH, CH), CH)
        return remote(out.at[0, rows], out.at[0, rows], po_s.at[c], po_r.at[c], mate)

    pair_hole = remote(
        acc.at[pl.ds(pl.multiple_of((1 - p) * HALF, HALF), HALF)], hx, ph_s, ph_r, mate)

    def meta_send():
        get_code_once()
        lax.fori_loop(0, NT, sort_meta, 0, unroll=4)
        x_meta_two().start()
        x_meta(0).start()
        x_meta(1).start()

    def meta_wait():
        x_meta_two().wait_recv()
        x_meta(0).wait_recv()
        x_meta(1).wait_recv()

    def amp_send(j):
        y_amp(j, 0).start()
        y_amp(j, 1).start()

    def amp_pass(j):
        y_amp(j, p).wait_recv()
        y_hop(j).start()

    def block_send(d):
        get_code_once()
        sort_blocks(d)
        send_blocks(d)

    def block_build(d):
        if "meta" not in ready:
            ready.add("meta")
            meta_wait()
        build_blocks(d)

    def hole_part(k):
        if "h" not in ready:
            ready.add("h")
            for g in get_h:
                g.wait()
        if k == 0:
            hole(0, amp_v, "acc" not in ready)
        elif k == 1:
            hole(3 - 2 * p, a_all.at[2 - 2 * p], "acc" not in ready)
        elif k == 2:
            for j in range(NP):
                y_amp(j, 1 - p).wait_recv()
            hole(1 + 2 * p, a_all.at[2 * p], "acc" not in ready)
        else:
            for j in range(NP):
                y_hop(j).wait_recv()
            hole(2, a_all.at[1], "acc" not in ready)
        ready.add("acc")

    def own():
        for c in range(NC):
            fin[crow(c), :] = product(c, 0)

    def finish(c):
        if "hx" not in ready:
            ready.add("hx")
            pair_hole.wait_recv()
        z_copy(0, 3, c).wait_recv()
        z_copy(1, 3, c).wait_recv()
        rows = pl.ds(pl.multiple_of(p * HALF + c * CH, CH), CH)
        total = fin[crow(c), :] + acc[rows, :] + hx[crow(c), :]
        total += zr[0, 3, crow(c), :].astype(F32) + zr[1, 3, crow(c), :].astype(F32)
        out[0, rows, :] = total.astype(BF16)
        pair_out(c).start()

    ready = set()

    def get_code_once():
        if "code" not in ready:
            ready.add("code")
            get_code.wait()
            get_lraw.wait()

    steps = {
        "META": meta_send, "YS": amp_send, "YP": amp_pass, "LS": block_send, "LH": hop_blocks,
        "LX": share_x, "LY": share_y, "LZ": share_pass, "LP": swap_blocks, "LB": block_build, "SS": send_sum, "SH": hop_sum, "Z": z_step,
        "HO": hole_part, "PH": pair_hole.start, "OP": own, "FIN": finish,
    }
    for c in range(NC):
        pair_amp(c).start()
    for g in get_h:
        g.start()
    get_amp.wait()
    for step in PLAN:
        steps[step[0]](*step[1:])

    pair_hole.wait_send()
    for i in range(2):
        x_meta(i).wait_send()
    for j in range(NP):
        y_amp(j, 0).wait_send()
        y_amp(j, 1).wait_send()
        y_hop(j).wait_send()
    x_meta_two().wait_send()

    for d in range(NZ):
        pair_block(d).wait_send()
        if d in SHARED:
            for dx in (1, 2, 3):
                x_share(d, dx).wait_send()
            y_share(d, 0).wait_send()
            y_share(d, 1).wait_send()
            y_share_hop(d).wait_send()
            continue
        x_block(d, 0).wait_send()
        x_block(d, 1).wait_send()
        if d not in DIRECT:
            x_via(d).wait_send()
        x_hop(d).wait_send()

    def drain_c(c, carry):
        pair_amp(c).wait_send()
        x_sum(c, 0).wait_send()
        x_sum(c, 1).wait_send()
        x_sum_hop(c).wait_send()
        for way in range(2):
            for h in range(4):
                z_copy(way, h, c).wait_send()
        pair_out(c).wait_send()
        other = pl.ds(pl.multiple_of((1 - p) * HALF + c * CH, CH), CH)
        remote(out.at[0, other], out.at[0, other], po_s.at[c], po_r.at[c], mate).wait_recv()
        return carry

    lax.fori_loop(0, NC, drain_c, 0)


def on_device(amplitudes, hh_integrals, ladder_blocks, block_target, block_live):
    dma = pltpu.SemaphoreType.DMA
    any_space = pl.BlockSpec(memory_space=pl.ANY)
    vmem = pl.BlockSpec(memory_space=pltpu.VMEM)
    return pl.pallas_call(
        kernel,
        out_shape=pltpu.VMEM((1, ROWS, COLS), BF16),
        in_specs=[any_space] * 5,
        out_specs=vmem,
        scratch_shapes=[
            pltpu.VMEM((ROWS, COLS), BF16),
            pltpu.VMEM((HALF, COLS), BF16),
            pltpu.VMEM((NX, HALF, COLS), BF16),
            pltpu.VMEM((NY - 1, ROWS, COLS), BF16),
            pltpu.VMEM((NY, ROWS, ROWS), BF16),
            pltpu.VMEM((NT, TILE, TILE), BF16),
            pltpu.VMEM((NZ, 2, NX, TILE, TILE), BF16),
            pltpu.VMEM((NZ, 2, NX - 1, TILE, TILE), BF16),
            pltpu.VMEM((NZ, TILE, TILE), BF16),
            pltpu.VMEM((NX, 4 * NZ, TILE), F32),
            pltpu.VMEM((NX - 1, 4 * NZ, TILE), F32),
            pltpu.VMEM((1, NT), jnp.int32),
            pltpu.VMEM((1, NT), jnp.int32),
            pltpu.VMEM((NT, TILE), jnp.int32),
            pltpu.SMEM((NT, TILE), jnp.int32),
            pltpu.VMEM((NZ, NX * COLS, COLS), BF16),
            pltpu.VMEM((2, 4, HALF, COLS), BF16),
            pltpu.VMEM((2, 4, HALF, COLS), BF16),
            pltpu.VMEM((ROWS, COLS), F32),
            pltpu.VMEM((HALF, COLS), F32),
            pltpu.VMEM((HALF, COLS), F32),
            dma, dma, dma, dma, dma, dma((NY,)),
            dma((NC,)), dma((NC,)),
            dma((NP, 3)), dma((NP, 3)),
            dma((NC, 3)), dma((NC, 3)),
            dma((NZ, 4)), dma((NZ, 4)),
            dma((NZ, 3)), dma((NZ, 3)),
            dma((3,)), dma((3,)),
            dma((NZ,)), dma((NZ,)),
            dma((2, 4, NC)), dma((2, 4, NC)),
            dma, dma,
            dma((NC,)), dma((NC,)),
        ],
        compiler_params=pltpu.CompilerParams(
            collective_id=0, has_side_effects=True, vmem_limit_bytes=56 * 2**20),
        cost_estimate=pl.CostEstimate(
            flops=4 * ROWS * 4096 * COLS, bytes_accessed=12 * 2**20, transcendentals=0),
        name="ladder_hole",
    )(block_target, block_live, amplitudes, hh_integrals, ladder_blocks)


def solution(mesh):
    return jax.shard_map(
        on_device,
        mesh=mesh,
        in_specs=(
            P("pair", "occ", "vir"),
            P("pair", "occ", None),
            P("vir", None, None, None),
            P("vir", None),
            P("vir", None),
        ),
        out_specs=P("pair", "occ", "vir"),
        check_vma=False,
    )
```
